32 devices in a mesh: tile: 16 (over z, x, core), tm: 2 (over y).
Axes of the slice: x: 2, y: 2, z: 4, core: 2. Of those that a mesh axis runs over, the one named last changes fastest.
Arguments:
- features: bfloat16 [192, 8, 16, 16, 128], P('tile', 'tm'), may hold values from -6 to 6
- weight_one: bfloat16 [3, 3, 128, 128], replicated, may hold values from -0.1875 to 0.1875
- bias_one: float32 [128], replicated, may hold values from -3 to 3
- weight_two: bfloat16 [3, 3, 128, 128], replicated, may hold values from -0.1875 to 0.1875
- bias_two: float32 [128], replicated, may hold values from -3 to 3
- cotangent: bfloat16 [192, 8, 16, 16, 128], P('tile', 'tm'), may hold values from -6 to 6
Outputs:
- output: bfloat16 [192, 8, 16, 16, 128], P('tile', 'tm')
- grad_weight_one: float32 [3, 3, 128, 128], replicated
- grad_bias_one: float32 [128], replicated
- grad_weight_two: float32 [3, 3, 128, 128], replicated
- grad_bias_two: float32 [128], replicated
The draws below stay inside these ranges and needn't reach their ends.
All inputs are finite; a program needn't handle non-finite values.
Results may differ from the reference program's by a relative error of at most 0.0085.
Values may be sent and summed in bfloat16 or wider, within the bound.
A program may use at most 256 MiB of HBM per device.

```python
import math
import jax
import jax.numpy as jnp
import numpy as np
from jax import lax

C = 128
S = 4
P_SIZE = 16
TILES = 192
NB = 8
PIXELS = 393216


def block_levels(own_key, shape, split, low, largest):
    factor_of = 1.0
    for dim, shards_of in split:
        draws = jax.random.uniform(jax.random.fold_in(jax.random.fold_in(own_key, 6), dim), (shards_of,), jnp.float32, low / len(split), largest / len(split))
        factor_of = factor_of * jnp.repeat(jnp.exp(draws), shape[dim] // shards_of).reshape((-1,) + (1,) * (len(shape) - 1 - dim))
    return factor_of


def noise(rng, dims, deviation, limit, shards=(), kind=jnp.bfloat16):
    drawn = deviation * jax.random.normal(rng, dims, jnp.float32)
    if shards:
        drawn = drawn * block_levels(rng, dims, shards, -0.22, 0.18)
    return jnp.clip(drawn, -limit, limit).astype(kind)


def setup_inputs(seed: int = 0) -> dict:
    arg_keys = jax.random.split(jax.random.key(seed), 7)
    features = noise(arg_keys[0], (TILES, NB, P_SIZE, P_SIZE, C), 1.0, 6.0, ((0, 16), (1, 2)))
    weight_one = noise(arg_keys[1], (3, 3, C, C), (9 * C) ** -0.5, 0.1875)
    bias_one = noise(arg_keys[2], (C,), 0.5, 3.0, (), jnp.float32)
    weight_two = noise(arg_keys[3], (3, 3, C, C), (9 * C) ** -0.5, 0.1875)
    bias_two = noise(arg_keys[4], (C,), 0.5, 3.0, (), jnp.float32)
    cotangent = noise(arg_keys[5], (TILES, NB, P_SIZE, P_SIZE, C), 1.0, 6.0, ((0, 16), (1, 2)))
    return {"features": features, "weight_one": weight_one, "bias_one": bias_one, "weight_two": weight_two, "bias_two": bias_two, "cotangent": cotangent}


inv_sqrt_two = 0.7071067811865476
inv_sqrt_tau = 0.3989422804014327

def edge_partner(face_id, edge_id):
    group_id = face_id // 4
    within = face_id % 4
    after_id = (within + 1) % 4
    before = (within + 3) % 4
    if group_id == 0:
        options = [(after_id, 2), (4 + within, 0), (before, 0), (4 + after_id, 2)]
    elif group_id == 1:
        options = [(within, 1), (8 + before, 0), (before, 3), (8 + within, 2)]
    else:
        options = [(4 + after_id, 1), (8 + before, 3), (4 + within, 3), (8 + after_id, 1)]
    return options[edge_id]

def entry_pixel(edge_id, along_edge, length):
    if edge_id == 0:
        return (0, along_edge)
    if edge_id == 1:
        return (length - 1, along_edge)
    if edge_id == 2:
        return (along_edge, 0)
    return (along_edge, length - 1)

def step_pixel(face_id, row_at, col_at, row_step, col_step, length):
    row_new = row_at + row_step
    col_new = col_at + col_step
    if 0 <= row_new < length and 0 <= col_new < length:
        return (face_id, row_new, col_new, -1)
    if row_new < 0:
        edge_id = 0
    elif row_new >= length:
        edge_id = 1
    elif col_new < 0:
        edge_id = 2
    else:
        edge_id = 3
    along_edge = col_at if edge_id < 2 else row_at
    partner, entered = edge_partner(face_id, edge_id)
    row_in, col_in = entry_pixel(entered, along_edge, length)
    return (partner, row_in, col_in, entered)

def neighbour_pixel(face_id, row_at, col_at, row_step, col_step, length):
    if row_step == 0 or col_step == 0:
        found = step_pixel(face_id, row_at, col_at, row_step, col_step, length)
        return (found[0], found[1], found[2])
    face_one, row_one, col_one, entered = step_pixel(face_id, row_at, col_at, row_step, 0, length)
    if entered >= 2:
        found = step_pixel(face_one, row_one, col_one, col_step, 0, length)
    else:
        found = step_pixel(face_one, row_one, col_one, 0, col_step, length)
    return (found[0], found[1], found[2])

def tile_slot(face_id, tile_row, tile_col, side_tiles):
    group_id = face_id // 4
    within = face_id % 4
    extra = 1 if group_id == 2 else 0
    column = (side_tiles * (within + extra) + tile_col) % (4 * side_tiles)
    return 3 * side_tiles * column + side_tiles * group_id + tile_row

def padding_tables(side_tiles, pixels):
    slot_count = 12 * side_tiles * side_tiles
    span = pixels + 2
    length = side_tiles * pixels
    index_map = np.zeros((slot_count, span, span), np.int64)
    outer_places = []
    outer_sources = []
    for face_id in range(12):
        for tile_row in range(side_tiles):
            for tile_col in range(side_tiles):
                slot_id = tile_slot(face_id, tile_row, tile_col, side_tiles)
                for row_at in range(-1, pixels + 1):
                    for col_at in range(-1, pixels + 1):
                        inner_row = min(max(row_at, 0), pixels - 1)
                        inner_col = min(max(col_at, 0), pixels - 1)
                        if row_at == inner_row and col_at == inner_col:
                            source = slot_id * pixels * pixels + row_at * pixels + col_at
                        else:
                            partner, row_new, col_new = neighbour_pixel(face_id, tile_row * pixels + inner_row, tile_col * pixels + inner_col, row_at - inner_row, col_at - inner_col, length)
                            source_slot = tile_slot(partner, row_new // pixels, col_new // pixels, side_tiles)
                            source = source_slot * pixels * pixels + row_new % pixels * pixels + col_new % pixels
                            outer_places.append(slot_id * span * span + (row_at + 1) * span + col_at + 1)
                            outer_sources.append(source)
                        index_map[slot_id, row_at + 1, col_at + 1] = source
    return (index_map.reshape(-1), np.array(outer_places, np.int64), np.array(outer_sources, np.int64))

def gelu_exact(value):
    return 0.5 * value * (1.0 + lax.erf(value * inv_sqrt_two))

def gelu_slope(value):
    return 0.5 * (1.0 + lax.erf(value * inv_sqrt_two)) + value * jnp.exp(-0.5 * value * value) * inv_sqrt_tau

def conv_columns(padded, pixels):
    pieces = []
    for row_off in range(3):
        for col_off in range(3):
            pieces.append(padded[..., row_off:row_off + pixels, col_off:col_off + pixels, :])
    joined = jnp.concatenate(pieces, axis=-1)
    return joined.reshape(-1, joined.shape[-1])

def spread_back(columns, lead, pixels, channels):
    parts = columns.reshape(lead + (pixels, pixels, 9, channels))
    total_sum = jnp.zeros(lead + (pixels + 2, pixels + 2, channels), jnp.float32)
    for row_off in range(3):
        for col_off in range(3):
            widths = [(0, 0)] * len(lead) + [(row_off, 2 - row_off), (col_off, 2 - col_off), (0, 0)]
            total_sum = total_sum + jnp.pad(parts[..., row_off * 3 + col_off, :], widths)
    return total_sum

def reference(features, weight_one, bias_one, weight_two, bias_two, cotangent):
    index_np, places_np, sources_np = padding_tables(S, P_SIZE)
    index_map = jnp.asarray(index_np).astype(jnp.int32)
    outer_places = jnp.asarray(places_np).astype(jnp.int32)
    outer_sources = jnp.asarray(sources_np).astype(jnp.int32)
    mat_one = weight_one.reshape(9 * C, C)
    mat_two = weight_two.reshape(9 * C, C)

    def pad_field(field_flat):
        return jnp.take(field_flat, index_map, axis=0).reshape(TILES, P_SIZE + 2, P_SIZE + 2, C)

    def fold_field(grad_pad):
        inner_part = grad_pad[:, 1:-1, 1:-1, :].reshape(-1, C)
        outer = jnp.take(grad_pad.reshape(-1, C), outer_places, axis=0).astype(jnp.bfloat16)
        outer = lax.optimization_barrier(outer)
        return inner_part.at[outer_sources].add(outer.astype(jnp.float32))

    def sample_step(carry, inputs):
        sample, cot_sample = inputs
        columns_one = conv_columns(pad_field(sample.reshape(-1, C)), P_SIZE)
        pre_one = jnp.dot(columns_one, mat_one, preferred_element_type=jnp.float32) + bias_one
        hidden = gelu_exact(pre_one).astype(jnp.bfloat16)
        columns_two = conv_columns(pad_field(hidden), P_SIZE)
        pre_two = jnp.dot(columns_two, mat_two, preferred_element_type=jnp.float32) + bias_two
        output = gelu_exact(pre_two).astype(jnp.bfloat16)
        delta_two = (cot_sample.reshape(-1, C).astype(jnp.float32) * gelu_slope(pre_two)).astype(jnp.bfloat16)
        grad_w_two = lax.dot_general(columns_two, delta_two, (((0,), (0,)), ((), ())), preferred_element_type=jnp.float32)
        grad_b_two = lax.optimization_barrier(jnp.sum(delta_two.astype(jnp.float32), axis=0))
        back_two = lax.dot_general(delta_two, mat_two, (((1,), (1,)), ((), ())), preferred_element_type=jnp.float32)
        grad_hidden = fold_field(spread_back(back_two, (TILES,), P_SIZE, C))
        delta_one = (grad_hidden * gelu_slope(pre_one)).astype(jnp.bfloat16)
        grad_w_one = lax.dot_general(columns_one, delta_one, (((0,), (0,)), ((), ())), preferred_element_type=jnp.float32)
        grad_b_one = lax.optimization_barrier(jnp.sum(delta_one.astype(jnp.float32), axis=0))
        carry = (carry[0] + grad_w_one, carry[1] + grad_b_one, carry[2] + grad_w_two, carry[3] + grad_b_two)
        return (carry, output.reshape(TILES, P_SIZE, P_SIZE, C))
    start = (jnp.zeros((9 * C, C), jnp.float32), jnp.zeros((C,), jnp.float32), jnp.zeros((9 * C, C), jnp.float32), jnp.zeros((C,), jnp.float32))
    carry, stacked = lax.scan(sample_step, start, (jnp.moveaxis(features, 1, 0), jnp.moveaxis(cotangent, 1, 0)))
    grad_scale = 1.0 / math.sqrt(PIXELS)
    output = jnp.moveaxis(stacked, 0, 1)
    return (output, (carry[0] * grad_scale).reshape(3, 3, C, C), carry[1] * grad_scale, (carry[2] * grad_scale).reshape(3, 3, C, C), carry[3] * grad_scale)
```

```python
import math

import jax
import jax.numpy as jnp
import numpy as np
from jax import lax
from jax.experimental import pallas as pl
from jax.experimental.pallas import tpu as pltpu
from jax.sharding import PartitionSpec as P

S = 4


inv_sqrt_two = 0.7071067811865476
inv_sqrt_tau = 0.3989422804014327


def passed_along(value, axis, steps):
    count = lax.axis_size(axis)
    pairs = [(source, (source + steps) % count) for source in range(count)]
    return lax.ppermute(value, axis, pairs)


def edge_partner(face_id, edge_id):
    group_id = face_id // 4
    within = face_id % 4
    after_id = (within + 1) % 4
    before = (within + 3) % 4
    if group_id == 0:
        options = [(after_id, 2), (4 + within, 0), (before, 0), (4 + after_id, 2)]
    elif group_id == 1:
        options = [(within, 1), (8 + before, 0), (before, 3), (8 + within, 2)]
    else:
        options = [(4 + after_id, 1), (8 + before, 3), (4 + within, 3), (8 + after_id, 1)]
    return options[edge_id]


def entry_pixel(edge_id, along_edge, length):
    if edge_id == 0:
        return (0, along_edge)
    if edge_id == 1:
        return (length - 1, along_edge)
    if edge_id == 2:
        return (along_edge, 0)
    return (along_edge, length - 1)


def step_pixel(face_id, row_at, col_at, row_step, col_step, length):
    row_new = row_at + row_step
    col_new = col_at + col_step
    if 0 <= row_new < length and 0 <= col_new < length:
        return (face_id, row_new, col_new, -1)
    if row_new < 0:
        edge_id = 0
    elif row_new >= length:
        edge_id = 1
    elif col_new < 0:
        edge_id = 2
    else:
        edge_id = 3
    along_edge = col_at if edge_id < 2 else row_at
    partner, entered = edge_partner(face_id, edge_id)
    row_in, col_in = entry_pixel(entered, along_edge, length)
    return (partner, row_in, col_in, entered)


def neighbour_pixel(face_id, row_at, col_at, row_step, col_step, length):
    if row_step == 0 or col_step == 0:
        found = step_pixel(face_id, row_at, col_at, row_step, col_step, length)
        return (found[0], found[1], found[2])
    face_one, row_one, col_one, entered = step_pixel(face_id, row_at, col_at, row_step, 0, length)
    if entered >= 2:
        found = step_pixel(face_one, row_one, col_one, col_step, 0, length)
    else:
        found = step_pixel(face_one, row_one, col_one, 0, col_step, length)
    return (found[0], found[1], found[2])


def tile_slot(face_id, tile_row, tile_col, side_tiles):
    group_id = face_id // 4
    within = face_id % 4
    extra = 1 if group_id == 2 else 0
    column = (side_tiles * (within + extra) + tile_col) % (4 * side_tiles)
    return 3 * side_tiles * column + side_tiles * group_id + tile_row


def cycle_position(row_at, col_at, pixels):
    if row_at == 0:
        return col_at
    if row_at == pixels - 1:
        return pixels + col_at
    if col_at == 0:
        return 2 * pixels + row_at
    return 3 * pixels + row_at


def halo_positions(pixels):
    places = [(-1, column) for column in range(-1, pixels + 1)]
    places = places + [(pixels, column) for column in range(-1, pixels + 1)]
    places = places + [(row_at, -1) for row_at in range(pixels)]
    places = places + [(row_at, pixels) for row_at in range(pixels)]
    return places


def halo_sources(side_tiles, pixels):
    slot_count = 12 * side_tiles * side_tiles
    places = halo_positions(pixels)
    length = side_tiles * pixels
    source_slot = np.zeros((slot_count, len(places)), np.int64)
    source_cycle = np.zeros((slot_count, len(places)), np.int64)
    for face_id in range(12):
        for tile_row in range(side_tiles):
            for tile_col in range(side_tiles):
                slot_id = tile_slot(face_id, tile_row, tile_col, side_tiles)
                for cell_index in range(len(places)):
                    row_at, col_at = places[cell_index]
                    inner_row = min(max(row_at, 0), pixels - 1)
                    inner_col = min(max(col_at, 0), pixels - 1)
                    partner, row_new, col_new = neighbour_pixel(
                        face_id,
                        tile_row * pixels + inner_row,
                        tile_col * pixels + inner_col,
                        row_at - inner_row,
                        col_at - inner_col,
                        length,
                    )
                    source_slot[slot_id, cell_index] = tile_slot(
                        partner, row_new // pixels, col_new // pixels, side_tiles
                    )
                    source_cycle[slot_id, cell_index] = cycle_position(
                        row_new % pixels, col_new % pixels, pixels
                    )
    return (source_slot, source_cycle)


def halo_rows(row_at, col_at, pixels):
    if row_at == -1 or row_at == pixels:
        base = 0 if row_at == -1 else 3 * pixels
        return [
            base + pixels * shift + col_at + 1 - shift
            for shift in range(3)
            if 0 <= col_at + 1 - shift < pixels
        ]
    return [6 * pixels + row_at if col_at == -1 else 7 * pixels + row_at]


def outer_row(row_at, col_at, pixels):
    if col_at == -1:
        return 2 * pixels + row_at + 1
    if col_at == pixels:
        return 4 * pixels + row_at + 1
    return col_at if row_at == -1 else pixels + col_at


def device_tables(device_count, per_device, side_tiles, pixels):
    source_slot, source_cycle = halo_sources(side_tiles, pixels)
    places = halo_positions(pixels)
    rim_len, halo_len, outer_len = 4 * pixels, 8 * pixels, 6 * pixels
    sends = {}
    local = []
    for device in range(device_count):
        local.append([])
        for local_id in range(per_device):
            slot_id = device * per_device + local_id
            for cell in range(len(places)):
                row_at, col_at = places[cell]
                source = int(source_slot[slot_id, cell])
                moved_by = (device - source // per_device) % device_count
                if moved_by > device_count // 2:
                    moved_by -= device_count
                rim = source % per_device * rim_len + int(source_cycle[slot_id, cell])
                halo = [local_id * halo_len + h for h in halo_rows(row_at, col_at, pixels)]
                outer = local_id * outer_len + outer_row(row_at, col_at, pixels)
                record = (rim, halo, outer)
                if moved_by == 0:
                    local[device].append(record)
                else:
                    lists = sends.setdefault(moved_by, [[] for _ in range(device_count)])
                    lists[device].append(record)
    offsets = sorted(sends)
    widths = [-(-max(len(one) for one in sends[offset]) // 16) * 16 for offset in offsets]
    total = sum(widths)
    send = np.full((device_count, total), -1, np.int32)
    receive = np.full((device_count, per_device * halo_len), -1, np.int32)
    back = np.full((device_count, total), -1, np.int32)
    target = np.full((device_count, per_device * outer_len + total), -1, np.int32)
    for device in range(device_count):
        for rim, halo, outer in local[device]:
            receive[device, halo] = rim
            target[device, outer] = rim
        base = 0
        for offset, width in zip(offsets, widths):
            sender = (device - offset) % device_count
            for at, (rim, halo, outer) in enumerate(sends[offset][device]):
                send[sender, base + at] = rim
                receive[device, halo] = per_device * rim_len + base + at
                back[device, base + at] = outer
                target[sender, per_device * outer_len + base + at] = rim
            base += width
    return (offsets, widths, send, receive, back, target)


def one_hot(table_np, tile_index, width):
    row = jnp.asarray(table_np, dtype=jnp.int32)[tile_index]
    return (row[:, None] == lax.broadcasted_iota(jnp.int32, (row.shape[0], width), 1)).astype(
        jnp.bfloat16
    )


def exchanged(rows, offsets, widths, sign):
    pieces, base = [], 0
    for offset, width in zip(offsets, widths):
        pieces.append(passed_along(rows[base : base + width], "tile", sign * offset))
        base += width
    return pieces


def halo_of(rim, layout, tile_index):
    offsets, widths, send, receive = layout[:4]
    outgoing = jnp.dot(one_hot(send, tile_index, rim.shape[0]), rim)
    pool = jnp.concatenate([rim] + exchanged(outgoing, offsets, widths, 1), axis=0)
    return jnp.dot(one_hot(receive, tile_index, pool.shape[0]), pool)


def folded(outer, layout, tile_index, rim_rows):
    offsets, widths, _, _, back, target = layout
    outgoing = jnp.dot(one_hot(back, tile_index, outer.shape[0]), outer)
    pool = jnp.concatenate([outer] + exchanged(outgoing, offsets, widths, -1), axis=0)
    spread = one_hot(target, tile_index, rim_rows)
    return lax.dot_general(
        spread, pool, (((0,), (0,)), ((), ())), preferred_element_type=jnp.float32
    )


def gelu_parts(value):
    half = 0.5 * (1.0 + lax.erf(value * inv_sqrt_two))
    return value * half, half + value * jnp.exp(-0.5 * value * value) * inv_sqrt_tau


def columns_at(tile, halo, work, pixels):
    count = pixels * pixels
    wide = tile.astype(jnp.float32)
    halo_wide = halo[6 * pixels :].astype(jnp.float32)
    work[0, pl.ds(1, count - 1), :] = wide[: count - 1]
    work[0, pl.ds(0, pixels, stride=pixels), :] = halo_wide[:pixels]
    work[1, pl.ds(0, count - 1), :] = wide[1:]
    work[1, pl.ds(pixels - 1, pixels, stride=pixels), :] = halo_wide[pixels:]
    middles = [work[0].astype(jnp.bfloat16), tile, work[1].astype(jnp.bfloat16)]
    joined = jnp.concatenate(
        [
            jnp.concatenate(
                [
                    halo[pixels * b : pixels * (b + 1)],
                    middles[b],
                    halo[pixels * (3 + b) : pixels * (4 + b)],
                ],
                axis=0,
            )
            for b in range(3)
        ],
        axis=1,
    )
    return jnp.concatenate([joined[pixels * a : pixels * a + count] for a in range(3)], axis=1)


def first_kernel(x_ref, halo_ref, w_ref, bias_ref, hidden_ref, slope_ref, rim_ref, work):
    batch, pixels, channels = x_ref.shape[1], x_ref.shape[2], x_ref.shape[4]
    count = pixels * pixels
    for s in range(batch):
        lanes = slice(s * channels, (s + 1) * channels)
        tile = x_ref[0, s].reshape(count, channels)
        cols = columns_at(tile, halo_ref[0, :, lanes], work.at[pl.ds(2 * s, 2)], pixels)
        pre = jnp.dot(cols, w_ref[...], preferred_element_type=jnp.float32) + bias_ref[...]
        hidden, slope = gelu_parts(pre)
        slope_ref[0, s] = slope
        work[2 * batch + s] = hidden
        rounded = hidden.astype(jnp.bfloat16)
        hidden_ref[0, s] = rounded.reshape(pixels, pixels, channels)
        rim_ref[0, 0:pixels, lanes] = rounded[:pixels]
        rim_ref[0, pixels : 2 * pixels, lanes] = rounded[count - pixels :]
        for side in range(2):
            edge = work[2 * batch + s, pl.ds(side * (pixels - 1), pixels, stride=pixels), :]
            rim_ref[0, (2 + side) * pixels : (3 + side) * pixels, lanes] = edge.astype(jnp.bfloat16)


def second_kernel(
    x_ref, halo_ref, cot_ref, w_ref, flip_ref, side_ref, bias_ref,
    out_ref, inner_ref, outer_ref, grad_ref, sum_ref, work, cols_ref, delta_ref, edge_ref,
):
    batch, pixels, channels = x_ref.shape[1], x_ref.shape[2], x_ref.shape[4]
    count = pixels * pixels

    @pl.when(pl.program_id(0) == 0)
    def _():
        grad_ref[...] = jnp.zeros_like(grad_ref)
        sum_ref[...] = jnp.zeros_like(sum_ref)

    zero_row = jnp.zeros((1, channels), jnp.float32)
    zero_col = jnp.zeros((pixels, channels), jnp.float32)
    zeros = jnp.zeros((2 * pixels, 3 * channels), jnp.bfloat16)
    for s in range(batch):
        lanes = slice(s * channels, (s + 1) * channels)
        tile = x_ref[0, s].reshape(count, channels)
        here = work.at[pl.ds(2 * s, 2)]
        cols = columns_at(tile, halo_ref[0, :, lanes], here, pixels)
        cols_ref[s * count : (s + 1) * count, :] = cols
        pre = jnp.dot(cols, w_ref[...], preferred_element_type=jnp.float32) + bias_ref[...]
        value, slope = gelu_parts(pre)
        out_ref[0, s] = value.astype(jnp.bfloat16).reshape(pixels, pixels, channels)
        cot = cot_ref[0, s].reshape(count, channels).astype(jnp.float32)
        delta = (cot * slope).astype(jnp.bfloat16)
        delta_ref[s * count : (s + 1) * count, :] = delta
        wide = delta.astype(jnp.float32)
        sum_ref[...] += jnp.sum(wide, axis=0, keepdims=True)
        edge_ref[s] = jnp.zeros(edge_ref.shape[1:], jnp.float32)
        work[2 * batch + s] = wide
        for side in range(2):
            edge_ref[s, side, pl.ds(2, pixels), :] = work[
                2 * batch + s, pl.ds(side * (pixels - 1), pixels, stride=pixels), :
            ]
        here[0, pl.ds(0, count - 1), :] = wide[1:]
        here[0, pl.ds(pixels - 1, pixels, stride=pixels), :] = zero_col
        here[1, pl.ds(1, count - 1), :] = wide[: count - 1]
        here[1, pl.ds(0, pixels, stride=pixels), :] = zero_col
        joined = jnp.concatenate(
            [here[0].astype(jnp.bfloat16), delta, here[1].astype(jnp.bfloat16)], axis=1
        )
        joined = jnp.concatenate([zeros, joined, zeros], axis=0)
        tall = count + 2 * pixels
        spread = jnp.concatenate(
            [joined[pixels * (2 - a) : pixels * (2 - a) + tall] for a in range(3)], axis=1
        )
        grad = jnp.dot(spread, flip_ref[...], preferred_element_type=jnp.float32)
        inner_ref[0, s] = grad[pixels : pixels + count]
        outer_ref[0, 0:pixels, lanes] = grad[:pixels].astype(jnp.bfloat16)
        outer_ref[0, pixels : 2 * pixels, lanes] = grad[pixels + count :].astype(jnp.bfloat16)
        for side in range(2):
            lhs = jnp.concatenate(
                [edge_ref[s, side, pl.ds(2 - a, 2 * pixels), :] for a in range(3)], axis=1
            ).astype(jnp.bfloat16)
            part = jnp.dot(lhs, side_ref[side], preferred_element_type=jnp.float32)
            outer_ref[0, 2 * pixels * (1 + side) : 2 * pixels * (2 + side), lanes] = part.astype(
                jnp.bfloat16
            )
    grad_ref[...] += lax.dot_general(
        delta_ref[...], cols_ref[...], (((0,), (0,)), ((), ())), preferred_element_type=jnp.float32
    )


def third_kernel(
    x_ref, halo_ref, inner_ref, rim_ref, slope_ref, grad_ref, sum_ref, work, cols_ref, delta_ref
):
    batch, pixels, channels = x_ref.shape[1], x_ref.shape[2], x_ref.shape[4]
    count = pixels * pixels

    @pl.when(pl.program_id(0) == 0)
    def _():
        grad_ref[...] = jnp.zeros_like(grad_ref)
        sum_ref[...] = jnp.zeros_like(sum_ref)

    for s in range(batch):
        lanes = slice(s * channels, (s + 1) * channels)
        tile = x_ref[0, s].reshape(count, channels)
        cols_ref[s * count : (s + 1) * count, :] = columns_at(
            tile, halo_ref[0, :, lanes], work.at[pl.ds(2 * s, 2)], pixels
        )
        at = 2 * batch + s
        work[at] = inner_ref[0, s]
        work[at, pl.ds(0, pixels), :] += rim_ref[0, 0:pixels, lanes]
        work[at, pl.ds(count - pixels, pixels), :] += rim_ref[0, pixels : 2 * pixels, lanes]
        for side in range(2):
            place = pl.ds(side * (pixels - 1), pixels, stride=pixels)
            edge = rim_ref[0, (2 + side) * pixels : (3 + side) * pixels, lanes]
            work[at, place, :] = work[at, place, :] + edge
        delta = (work[at] * slope_ref[0, s]).astype(jnp.bfloat16)
        delta_ref[s * count : (s + 1) * count, :] = delta
        sum_ref[...] += jnp.sum(delta.astype(jnp.float32), axis=0, keepdims=True)
    grad_ref[...] += lax.dot_general(
        delta_ref[...], cols_ref[...], (((0,), (0,)), ((), ())), preferred_element_type=jnp.float32
    )


def per_tile(shape):
    return pl.BlockSpec((1,) + tuple(shape), lambda t: (t,) + (0,) * len(shape))


def whole(shape):
    return pl.BlockSpec(tuple(shape), lambda t: (0,) * len(shape))


params = dict(vmem_limit_bytes=48 * 1024 * 1024)


def body(features, weight_one, bias_one, weight_two, bias_two, cotangent):
    device_count = lax.axis_size("tile")
    samples_count = lax.axis_size("tm")
    tile_index = lax.axis_index("tile")
    per_device, batch, pixels, _, channels = features.shape
    count = pixels * pixels
    lane_count = batch * channels
    layout = device_tables(device_count, per_device, S, pixels)
    bf16, f32 = jnp.bfloat16, jnp.float32
    tile_shape = (batch, pixels, pixels, channels)
    flat_shape = (batch, count, channels)
    halo_shape = (8 * pixels, lane_count)
    rim_shape = (4 * pixels, lane_count)
    outer_shape = (6 * pixels, lane_count)
    mat_one = weight_one.reshape(9 * channels, channels)
    mat_two = weight_two.reshape(9 * channels, channels)
    turned = weight_two.transpose(0, 1, 3, 2)
    flip = turned.reshape(9 * channels, channels)
    sides = jnp.stack([turned[:, 0], turned[:, 2]]).reshape(2, 3 * channels, channels)

    def out(shape, dtype):
        return jax.ShapeDtypeStruct((per_device,) + tuple(shape), dtype)

    work = pltpu.VMEM((3 * batch, count, channels), f32)
    cols = pltpu.VMEM((batch * count, 9 * channels), bf16)
    deltas = pltpu.VMEM((batch * count, channels), bf16)
    grad_shape = (channels, 9 * channels)

    rim_one = jnp.concatenate(
        [features[:, :, 0], features[:, :, -1], features[:, :, :, 0], features[:, :, :, -1]], axis=2
    )
    rim_one = rim_one.transpose(0, 2, 1, 3).reshape(per_device * 4 * pixels, lane_count)
    halo_one = halo_of(rim_one, layout, tile_index).reshape((per_device,) + halo_shape)
    hidden, slope, rim_two = pl.pallas_call(
        first_kernel,
        grid=(per_device,),
        in_specs=[per_tile(tile_shape), per_tile(halo_shape), whole(mat_one.shape), whole((1, channels))],
        out_specs=[per_tile(tile_shape), per_tile(flat_shape), per_tile(rim_shape)],
        out_shape=[out(tile_shape, bf16), out(flat_shape, f32), out(rim_shape, bf16)],
        scratch_shapes=[work],
        compiler_params=pltpu.CompilerParams(**params),
    )(features, halo_one, mat_one, bias_one.reshape(1, channels))
    halo_two = halo_of(rim_two.reshape(-1, lane_count), layout, tile_index)
    output, inner, outer, grad_two, sum_two = pl.pallas_call(
        second_kernel,
        grid=(per_device,),
        in_specs=[
            per_tile(tile_shape), per_tile(halo_shape), per_tile(tile_shape), whole(mat_two.shape),
            whole(flip.shape), whole(sides.shape), whole((1, channels)),
        ],
        out_specs=[
            per_tile(tile_shape), per_tile(flat_shape), per_tile(outer_shape),
            whole(grad_shape), whole((1, channels)),
        ],
        out_shape=[
            out(tile_shape, bf16), out(flat_shape, f32), out(outer_shape, bf16),
            jax.ShapeDtypeStruct(grad_shape, f32), jax.ShapeDtypeStruct((1, channels), f32),
        ],
        scratch_shapes=[work, cols, deltas, pltpu.VMEM((batch, 2, 2 * pixels + 8, channels), f32)],
        compiler_params=pltpu.CompilerParams(**params),
    )(
        hidden, halo_two.reshape((per_device,) + halo_shape), cotangent, mat_two, flip, sides,
        bias_two.reshape(1, channels),
    )
    rim_grad = folded(outer.reshape(-1, lane_count), layout, tile_index, per_device * 4 * pixels)
    grad_one, sum_one = pl.pallas_call(
        third_kernel,
        grid=(per_device,),
        in_specs=[
            per_tile(tile_shape), per_tile(halo_shape), per_tile(flat_shape), per_tile(rim_shape),
            per_tile(flat_shape),
        ],
        out_specs=[whole(grad_shape), whole((1, channels))],
        out_shape=[jax.ShapeDtypeStruct(grad_shape, f32), jax.ShapeDtypeStruct((1, channels), f32)],
        scratch_shapes=[work, cols, deltas],
        compiler_params=pltpu.CompilerParams(**params),
    )(features, halo_one, inner, rim_grad.reshape((per_device,) + rim_shape), slope)

    total_pixels = 12 * S * S * count * batch * samples_count
    grad_scale = 1.0 / math.sqrt(total_pixels)
    devices = device_count * samples_count
    axes = ("tile", "tm")

    def summed(grad, bias):
        rows = jnp.concatenate([grad.reshape(-1, channels), bias], axis=0)
        used = rows.shape[0]
        chunk = -(-used // (8 * devices)) * 8
        rows = jnp.pad(rows, ((0, chunk * devices - used), (0, 0)))
        parts = lax.all_to_all(rows.reshape(devices, chunk, channels), axes, 0, 0)
        mine = jnp.sum(parts, axis=0) * grad_scale
        total = lax.all_gather(mine, axes, axis=0, tiled=True)
        weight = total[: used - 1].reshape(channels, 3, 3, channels).transpose(1, 2, 3, 0)
        return weight, total[used - 1]

    grad_weight_two, grad_bias_two = summed(grad_two, sum_two)
    grad_weight_one, grad_bias_one = summed(grad_one, sum_one)
    return (output, grad_weight_one, grad_bias_one, grad_weight_two, grad_bias_two)


def solution(mesh):
    return jax.shard_map(
        body,
        mesh=mesh,
        in_specs=(
            P("tile", "tm", None, None, None),
            P(),
            P(),
            P(),
            P(),
            P("tile", "tm", None, None, None),
        ),
        out_specs=(P("tile", "tm", None, None, None), P(), P(), P(), P()),
        check_vma=False,
    )
```

```python
import math

import jax
import jax.numpy as jnp
import numpy as np
from jax import lax
from jax.experimental import pallas as pl
from jax.experimental.pallas import tpu as pltpu
from jax.sharding import PartitionSpec as P

S = 4


inv_sqrt_two = 0.7071067811865476
inv_sqrt_tau = 0.3989422804014327


def passed_along(value, axis, steps):
    count = lax.axis_size(axis)
    pairs = [(source, (source + steps) % count) for source in range(count)]
    return lax.ppermute(value, axis, pairs)


def edge_partner(face_id, edge_id):
    group_id = face_id // 4
    within = face_id % 4
    after_id = (within + 1) % 4
    before = (within + 3) % 4
    if group_id == 0:
        options = [(after_id, 2), (4 + within, 0), (before, 0), (4 + after_id, 2)]
    elif group_id == 1:
        options = [(within, 1), (8 + before, 0), (before, 3), (8 + within, 2)]
    else:
        options = [(4 + after_id, 1), (8 + before, 3), (4 + within, 3), (8 + after_id, 1)]
    return options[edge_id]


def entry_pixel(edge_id, along_edge, length):
    if edge_id == 0:
        return (0, along_edge)
    if edge_id == 1:
        return (length - 1, along_edge)
    if edge_id == 2:
        return (along_edge, 0)
    return (along_edge, length - 1)


def step_pixel(face_id, row_at, col_at, row_step, col_step, length):
    row_new = row_at + row_step
    col_new = col_at + col_step
    if 0 <= row_new < length and 0 <= col_new < length:
        return (face_id, row_new, col_new, -1)
    if row_new < 0:
        edge_id = 0
    elif row_new >= length:
        edge_id = 1
    elif col_new < 0:
        edge_id = 2
    else:
        edge_id = 3
    along_edge = col_at if edge_id < 2 else row_at
    partner, entered = edge_partner(face_id, edge_id)
    row_in, col_in = entry_pixel(entered, along_edge, length)
    return (partner, row_in, col_in, entered)


def neighbour_pixel(face_id, row_at, col_at, row_step, col_step, length):
    if row_step == 0 or col_step == 0:
        found = step_pixel(face_id, row_at, col_at, row_step, col_step, length)
        return (found[0], found[1], found[2])
    face_one, row_one, col_one, entered = step_pixel(face_id, row_at, col_at, row_step, 0, length)
    if entered >= 2:
        found = step_pixel(face_one, row_one, col_one, col_step, 0, length)
    else:
        found = step_pixel(face_one, row_one, col_one, 0, col_step, length)
    return (found[0], found[1], found[2])


def tile_slot(face_id, tile_row, tile_col, side_tiles):
    group_id = face_id // 4
    within = face_id % 4
    extra = 1 if group_id == 2 else 0
    column = (side_tiles * (within + extra) + tile_col) % (4 * side_tiles)
    return 3 * side_tiles * column + side_tiles * group_id + tile_row


def cycle_position(row_at, col_at, pixels):
    if row_at == 0:
        return col_at
    if row_at == pixels - 1:
        return pixels + col_at
    if col_at == 0:
        return 2 * pixels + row_at
    return 3 * pixels + row_at


def halo_positions(pixels):
    places = [(-1, column) for column in range(-1, pixels + 1)]
    places = places + [(pixels, column) for column in range(-1, pixels + 1)]
    places = places + [(row_at, -1) for row_at in range(pixels)]
    places = places + [(row_at, pixels) for row_at in range(pixels)]
    return places


def halo_sources(side_tiles, pixels):
    slot_count = 12 * side_tiles * side_tiles
    places = halo_positions(pixels)
    length = side_tiles * pixels
    source_slot = np.zeros((slot_count, len(places)), np.int64)
    source_cycle = np.zeros((slot_count, len(places)), np.int64)
    for face_id in range(12):
        for tile_row in range(side_tiles):
            for tile_col in range(side_tiles):
                slot_id = tile_slot(face_id, tile_row, tile_col, side_tiles)
                for cell_index in range(len(places)):
                    row_at, col_at = places[cell_index]
                    inner_row = min(max(row_at, 0), pixels - 1)
                    inner_col = min(max(col_at, 0), pixels - 1)
                    partner, row_new, col_new = neighbour_pixel(
                        face_id,
                        tile_row * pixels + inner_row,
                        tile_col * pixels + inner_col,
                        row_at - inner_row,
                        col_at - inner_col,
                        length,
                    )
                    source_slot[slot_id, cell_index] = tile_slot(
                        partner, row_new // pixels, col_new // pixels, side_tiles
                    )
                    source_cycle[slot_id, cell_index] = cycle_position(
                        row_new % pixels, col_new % pixels, pixels
                    )
    return (source_slot, source_cycle)


def halo_rows(row_at, col_at, pixels):
    if row_at == -1 or row_at == pixels:
        base = 0 if row_at == -1 else 3 * pixels
        return [
            base + pixels * shift + col_at + 1 - shift
            for shift in range(3)
            if 0 <= col_at + 1 - shift < pixels
        ]
    return [6 * pixels + row_at if col_at == -1 else 7 * pixels + row_at]


def outer_row(row_at, col_at, pixels):
    if col_at == -1:
        return 2 * pixels + row_at + 1
    if col_at == pixels:
        return 4 * pixels + row_at + 1
    return col_at if row_at == -1 else pixels + col_at


def device_tables(device_count, per_device, side_tiles, pixels):
    source_slot, source_cycle = halo_sources(side_tiles, pixels)
    places = halo_positions(pixels)
    rim_len, halo_len, outer_len = 4 * pixels, 8 * pixels, 6 * pixels
    sends = {}
    local = []
    for device in range(device_count):
        local.append([])
        for local_id in range(per_device):
            slot_id = device * per_device + local_id
            for cell in range(len(places)):
                row_at, col_at = places[cell]
                source = int(source_slot[slot_id, cell])
                moved_by = (device - source // per_device) % device_count
                if moved_by > device_count // 2:
                    moved_by -= device_count
                rim = source % per_device * rim_len + int(source_cycle[slot_id, cell])
                halo = [local_id * halo_len + h for h in halo_rows(row_at, col_at, pixels)]
                outer = local_id * outer_len + outer_row(row_at, col_at, pixels)
                record = (rim, halo, outer)
                if moved_by == 0:
                    local[device].append(record)
                else:
                    lists = sends.setdefault(moved_by, [[] for _ in range(device_count)])
                    lists[device].append(record)
    offsets = sorted(sends)
    widths = [-(-max(len(one) for one in sends[offset]) // 16) * 16 for offset in offsets]
    total = sum(widths)
    send = np.full((device_count, total), -1, np.int32)
    receive = np.full((device_count, per_device * halo_len), -1, np.int32)
    back = np.full((device_count, total), -1, np.int32)
    target = np.full((device_count, per_device * outer_len + total), -1, np.int32)
    for device in range(device_count):
        for rim, halo, outer in local[device]:
            receive[device, halo] = rim
            target[device, outer] = rim
        base = 0
        for offset, width in zip(offsets, widths):
            sender = (device - offset) % device_count
            for at, (rim, halo, outer) in enumerate(sends[offset][device]):
                send[sender, base + at] = rim
                receive[device, halo] = per_device * rim_len + base + at
                back[device, base + at] = outer
                target[sender, per_device * outer_len + base + at] = rim
            base += width
    return (offsets, widths, send, receive, back, target)


def one_hot(table_np, tile_index, width):
    row = jnp.asarray(table_np, dtype=jnp.int32)[tile_index]
    return (row[:, None] == lax.broadcasted_iota(jnp.int32, (row.shape[0], width), 1)).astype(
        jnp.bfloat16
    )


def exchanged(rows, offsets, widths, sign):
    pieces, base = [], 0
    for offset, width in zip(offsets, widths):
        pieces.append(passed_along(rows[base : base + width], "tile", sign * offset))
        base += width
    return pieces


def halo_of(rim, layout, tile_index):
    offsets, widths, send, receive = layout[:4]
    outgoing = jnp.dot(one_hot(send, tile_index, rim.shape[0]), rim)
    pool = jnp.concatenate([rim] + exchanged(outgoing, offsets, widths, 1), axis=0)
    return jnp.dot(one_hot(receive, tile_index, pool.shape[0]), pool)


def folded(outer, layout, tile_index, rim_rows):
    offsets, widths, _, _, back, target = layout
    outgoing = jnp.dot(one_hot(back, tile_index, outer.shape[0]), outer)
    pool = jnp.concatenate([outer] + exchanged(outgoing, offsets, widths, -1), axis=0)
    spread = one_hot(target, tile_index, rim_rows)
    return lax.dot_general(
        spread, pool, (((0,), (0,)), ((), ())), preferred_element_type=jnp.float32
    )


def gelu_parts(value):
    half = 0.5 * (1.0 + lax.erf(value * inv_sqrt_two))
    return value * half, half + value * jnp.exp(-0.5 * value * value) * inv_sqrt_tau


def columns_at(tile, halo, work, pixels):
    count = pixels * pixels
    wide = tile.astype(jnp.float32)
    halo_wide = halo[6 * pixels :].astype(jnp.float32)
    work[0, pl.ds(1, count - 1), :] = wide[: count - 1]
    work[0, pl.ds(0, pixels, stride=pixels), :] = halo_wide[:pixels]
    work[1, pl.ds(0, count - 1), :] = wide[1:]
    work[1, pl.ds(pixels - 1, pixels, stride=pixels), :] = halo_wide[pixels:]
    middles = [work[0].astype(jnp.bfloat16), tile, work[1].astype(jnp.bfloat16)]
    joined = jnp.concatenate(
        [
            jnp.concatenate(
                [
                    halo[pixels * b : pixels * (b + 1)],
                    middles[b],
                    halo[pixels * (3 + b) : pixels * (4 + b)],
                ],
                axis=0,
            )
            for b in range(3)
        ],
        axis=1,
    )
    return jnp.concatenate([joined[pixels * a : pixels * a + count] for a in range(3)], axis=1)


def first_kernel(x_ref, halo_ref, w_ref, bias_ref, hidden_ref, slope_ref, rim_ref, work):
    batch, pixels, channels = x_ref.shape[1], x_ref.shape[2], x_ref.shape[4]
    count = pixels * pixels
    for s in range(batch):
        lanes = slice(s * channels, (s + 1) * channels)
        tile = x_ref[0, s].reshape(count, channels)
        cols = columns_at(tile, halo_ref[0, :, lanes], work.at[pl.ds(2 * s, 2)], pixels)
        pre = jnp.dot(cols, w_ref[...], preferred_element_type=jnp.float32) + bias_ref[...]
        hidden, slope = gelu_parts(pre)
        slope_ref[0, s] = slope
        work[2 * batch + s] = hidden
        rounded = hidden.astype(jnp.bfloat16)
        hidden_ref[0, s] = rounded.reshape(pixels, pixels, channels)
        rim_ref[0, 0:pixels, lanes] = rounded[:pixels]
        rim_ref[0, pixels : 2 * pixels, lanes] = rounded[count - pixels :]
        for side in range(2):
            edge = work[2 * batch + s, pl.ds(side * (pixels - 1), pixels, stride=pixels), :]
            rim_ref[0, (2 + side) * pixels : (3 + side) * pixels, lanes] = edge.astype(jnp.bfloat16)


def second_kernel(
    x_ref, halo_ref, cot_ref, w_ref, flip_ref, side_ref, bias_ref,
    out_ref, inner_ref, outer_ref, grad_ref, sum_ref, work, cols_ref, delta_ref, edge_ref,
):
    batch, pixels, channels = x_ref.shape[1], x_ref.shape[2], x_ref.shape[4]
    count = pixels * pixels

    @pl.when(pl.program_id(0) == 0)
    def _():
        grad_ref[...] = jnp.zeros_like(grad_ref)
        sum_ref[...] = jnp.zeros_like(sum_ref)

    zero_row = jnp.zeros((1, channels), jnp.float32)
    zero_col = jnp.zeros((pixels, channels), jnp.float32)
    zeros = jnp.zeros((2 * pixels, 3 * channels), jnp.bfloat16)
    for s in range(batch):
        lanes = slice(s * channels, (s + 1) * channels)
        tile = x_ref[0, s].reshape(count, channels)
        here = work.at[pl.ds(2 * s, 2)]
        cols = columns_at(tile, halo_ref[0, :, lanes], here, pixels)
        cols_ref[s * count : (s + 1) * count, :] = cols
        pre = jnp.dot(cols, w_ref[...], preferred_element_type=jnp.float32) + bias_ref[...]
        value, slope = gelu_parts(pre)
        out_ref[0, s] = value.astype(jnp.bfloat16).reshape(pixels, pixels, channels)
        cot = cot_ref[0, s].reshape(count, channels).astype(jnp.float32)
        delta = (cot * slope).astype(jnp.bfloat16)
        delta_ref[s * count : (s + 1) * count, :] = delta
        wide = delta.astype(jnp.float32)
        sum_ref[...] += jnp.sum(wide, axis=0, keepdims=True)
        edge_ref[s] = jnp.zeros(edge_ref.shape[1:], jnp.float32)
        work[2 * batch + s] = wide
        for side in range(2):
            edge_ref[s, side, pl.ds(2, pixels), :] = work[
                2 * batch + s, pl.ds(side * (pixels - 1), pixels, stride=pixels), :
            ]
        here[0, pl.ds(0, count - 1), :] = wide[1:]
        here[0, pl.ds(pixels - 1, pixels, stride=pixels), :] = zero_col
        here[1, pl.ds(1, count - 1), :] = wide[: count - 1]
        here[1, pl.ds(0, pixels, stride=pixels), :] = zero_col
        joined = jnp.concatenate(
            [here[0].astype(jnp.bfloat16), delta, here[1].astype(jnp.bfloat16)], axis=1
        )
        joined = jnp.concatenate([zeros, joined, zeros], axis=0)
        tall = count + 2 * pixels
        spread = jnp.concatenate(
            [joined[pixels * (2 - a) : pixels * (2 - a) + tall] for a in range(3)], axis=1
        )
        grad = jnp.dot(spread, flip_ref[...], preferred_element_type=jnp.float32)
        inner_ref[0, s] = grad[pixels : pixels + count]
        outer_ref[0, 0:pixels, lanes] = grad[:pixels].astype(jnp.bfloat16)
        outer_ref[0, pixels : 2 * pixels, lanes] = grad[pixels + count :].astype(jnp.bfloat16)
        for side in range(2):
            lhs = jnp.concatenate(
                [edge_ref[s, side, pl.ds(2 - a, 2 * pixels), :] for a in range(3)], axis=1
            ).astype(jnp.bfloat16)
            part = jnp.dot(lhs, side_ref[side], preferred_element_type=jnp.float32)
            outer_ref[0, 2 * pixels * (1 + side) : 2 * pixels * (2 + side), lanes] = part.astype(
                jnp.bfloat16
            )
    grad_ref[...] += lax.dot_general(
        delta_ref[...], cols_ref[...], (((0,), (0,)), ((), ())), preferred_element_type=jnp.float32
    )


def third_kernel(
    x_ref, halo_ref, inner_ref, rim_ref, slope_ref, grad_ref, sum_ref, work, cols_ref, delta_ref
):
    batch, pixels, channels = x_ref.shape[1], x_ref.shape[2], x_ref.shape[4]
    count = pixels * pixels

    @pl.when(pl.program_id(0) == 0)
    def _():
        grad_ref[...] = jnp.zeros_like(grad_ref)
        sum_ref[...] = jnp.zeros_like(sum_ref)

    for s in range(batch):
        lanes = slice(s * channels, (s + 1) * channels)
        tile = x_ref[0, s].reshape(count, channels)
        cols_ref[s * count : (s + 1) * count, :] = columns_at(
            tile, halo_ref[0, :, lanes], work.at[pl.ds(2 * s, 2)], pixels
        )
        at = 2 * batch + s
        work[at] = inner_ref[0, s]
        work[at, pl.ds(0, pixels), :] += rim_ref[0, 0:pixels, lanes]
        work[at, pl.ds(count - pixels, pixels), :] += rim_ref[0, pixels : 2 * pixels, lanes]
        for side in range(2):
            place = pl.ds(side * (pixels - 1), pixels, stride=pixels)
            edge = rim_ref[0, (2 + side) * pixels : (3 + side) * pixels, lanes]
            work[at, place, :] = work[at, place, :] + edge
        delta = (work[at] * slope_ref[0, s]).astype(jnp.bfloat16)
        delta_ref[s * count : (s + 1) * count, :] = delta
        sum_ref[...] += jnp.sum(delta.astype(jnp.float32), axis=0, keepdims=True)
    grad_ref[...] += lax.dot_general(
        delta_ref[...], cols_ref[...], (((0,), (0,)), ((), ())), preferred_element_type=jnp.float32
    )


def per_tile(shape):
    return pl.BlockSpec((1,) + tuple(shape), lambda t: (t,) + (0,) * len(shape))


def whole(shape):
    return pl.BlockSpec(tuple(shape), lambda t: (0,) * len(shape))


params = dict(vmem_limit_bytes=48 * 1024 * 1024)


def body(features, weight_one, bias_one, weight_two, bias_two, cotangent):
    device_count = lax.axis_size("tile")
    samples_count = lax.axis_size("tm")
    tile_index = lax.axis_index("tile")
    per_device, batch, pixels, _, channels = features.shape
    count = pixels * pixels
    lane_count = batch * channels
    layout = device_tables(device_count, per_device, S, pixels)
    bf16, f32 = jnp.bfloat16, jnp.float32
    tile_shape = (batch, pixels, pixels, channels)
    flat_shape = (batch, count, channels)
    halo_shape = (8 * pixels, lane_count)
    rim_shape = (4 * pixels, lane_count)
    outer_shape = (6 * pixels, lane_count)
    mat_one = weight_one.reshape(9 * channels, channels)
    mat_two = weight_two.reshape(9 * channels, channels)
    turned = weight_two.transpose(0, 1, 3, 2)
    flip = turned.reshape(9 * channels, channels)
    sides = jnp.stack([turned[:, 0], turned[:, 2]]).reshape(2, 3 * channels, channels)

    def out(shape, dtype):
        return jax.ShapeDtypeStruct((per_device,) + tuple(shape), dtype)

    work = pltpu.VMEM((3 * batch, count, channels), f32)
    cols = pltpu.VMEM((batch * count, 9 * channels), bf16)
    deltas = pltpu.VMEM((batch * count, channels), bf16)
    grad_shape = (channels, 9 * channels)

    rim_one = jnp.concatenate(
        [features[:, :, 0], features[:, :, -1], features[:, :, :, 0], features[:, :, :, -1]], axis=2
    )
    rim_one = rim_one.transpose(0, 2, 1, 3).reshape(per_device * 4 * pixels, lane_count)
    halo_one = halo_of(rim_one, layout, tile_index).reshape((per_device,) + halo_shape)
    hidden, slope, rim_two = pl.pallas_call(
        first_kernel,
        grid=(per_device,),
        in_specs=[per_tile(tile_shape), per_tile(halo_shape), whole(mat_one.shape), whole((1, channels))],
        out_specs=[per_tile(tile_shape), per_tile(flat_shape), per_tile(rim_shape)],
        out_shape=[out(tile_shape, bf16), out(flat_shape, f32), out(rim_shape, bf16)],
        scratch_shapes=[work],
        compiler_params=pltpu.CompilerParams(**params),
    )(features, halo_one, mat_one, bias_one.reshape(1, channels))
    halo_two = halo_of(rim_two.reshape(-1, lane_count), layout, tile_index)
    output, inner, outer, grad_two, sum_two = pl.pallas_call(
        second_kernel,
        grid=(per_device,),
        in_specs=[
            per_tile(tile_shape), per_tile(halo_shape), per_tile(tile_shape), whole(mat_two.shape),
            whole(flip.shape), whole(sides.shape), whole((1, channels)),
        ],
        out_specs=[
            per_tile(tile_shape), per_tile(flat_shape), per_tile(outer_shape),
            whole(grad_shape), whole((1, channels)),
        ],
        out_shape=[
            out(tile_shape, bf16), out(flat_shape, f32), out(outer_shape, bf16),
            jax.ShapeDtypeStruct(grad_shape, f32), jax.ShapeDtypeStruct((1, channels), f32),
        ],
        scratch_shapes=[work, cols, deltas, pltpu.VMEM((batch, 2, 2 * pixels + 8, channels), f32)],
        compiler_params=pltpu.CompilerParams(**params),
    )(
        hidden, halo_two.reshape((per_device,) + halo_shape), cotangent, mat_two, flip, sides,
        bias_two.reshape(1, channels),
    )
    rim_grad = folded(outer.reshape(-1, lane_count), layout, tile_index, per_device * 4 * pixels)
    grad_one, sum_one = pl.pallas_call(
        third_kernel,
        grid=(per_device,),
        in_specs=[
            per_tile(tile_shape), per_tile(halo_shape), per_tile(flat_shape), per_tile(rim_shape),
            per_tile(flat_shape),
        ],
        out_specs=[whole(grad_shape), whole((1, channels))],
        out_shape=[jax.ShapeDtypeStruct(grad_shape, f32), jax.ShapeDtypeStruct((1, channels), f32)],
        scratch_shapes=[work, cols, deltas],
        compiler_params=pltpu.CompilerParams(**params),
    )(features, halo_one, inner, rim_grad.reshape((per_device,) + rim_shape), slope)

    total_pixels = 12 * S * S * count * batch * samples_count
    grad_scale = 1.0 / math.sqrt(total_pixels)
    devices = device_count * samples_count
    axes = ("tile", "tm")

    rows = jnp.concatenate(
        [grad_one.reshape(-1, channels), sum_one, grad_two.reshape(-1, channels), sum_two], axis=0
    )
    used = rows.shape[0]
    chunk = -(-used // (8 * devices)) * 8
    rows = jnp.pad(rows, ((0, chunk * devices - used), (0, 0)))
    parts = lax.all_to_all(rows.reshape(devices, chunk, channels), axes, 0, 0)
    mine = jnp.sum(parts, axis=0) * grad_scale
    copies = jnp.broadcast_to(mine[None], (devices, chunk, channels))
    total = lax.all_to_all(copies, axes, 0, 0).reshape(devices * chunk, channels)

    def unpacked(part):
        weight = part[:-1].reshape(channels, 3, 3, channels).transpose(1, 2, 3, 0)
        return weight, part[-1]

    grad_weight_one, grad_bias_one = unpacked(total[: used // 2])
    grad_weight_two, grad_bias_two = unpacked(total[used // 2 : used])
    return (output, grad_weight_one, grad_bias_one, grad_weight_two, grad_bias_two)


def solution(mesh):
    return jax.shard_map(
        body,
        mesh=mesh,
        in_specs=(
            P("tile", "tm", None, None, None),
            P(),
            P(),
            P(),
            P(),
            P("tile", "tm", None, None, None),
        ),
        out_specs=(P("tile", "tm", None, None, None), P(), P(), P(), P()),
        check_vma=False,
    )
```

```python
import math

import jax
import jax.numpy as jnp
import numpy as np
from jax import lax
from jax.experimental import pallas as pl
from jax.experimental.pallas import tpu as pltpu
from jax.sharding import PartitionSpec as P

S = 4


inv_sqrt_two = 0.7071067811865476
inv_sqrt_tau = 0.3989422804014327


def passed_along(value, axis, steps):
    count = lax.axis_size(axis)
    pairs = [(source, (source + steps) % count) for source in range(count)]
    return lax.ppermute(value, axis, pairs)


def edge_partner(face_id, edge_id):
    group_id = face_id // 4
    within = face_id % 4
    after_id = (within + 1) % 4
    before = (within + 3) % 4
    if group_id == 0:
        options = [(after_id, 2), (4 + within, 0), (before, 0), (4 + after_id, 2)]
    elif group_id == 1:
        options = [(within, 1), (8 + before, 0), (before, 3), (8 + within, 2)]
    else:
        options = [(4 + after_id, 1), (8 + before, 3), (4 + within, 3), (8 + after_id, 1)]
    return options[edge_id]


def entry_pixel(edge_id, along_edge, length):
    if edge_id == 0:
        return (0, along_edge)
    if edge_id == 1:
        return (length - 1, along_edge)
    if edge_id == 2:
        return (along_edge, 0)
    return (along_edge, length - 1)


def step_pixel(face_id, row_at, col_at, row_step, col_step, length):
    row_new = row_at + row_step
    col_new = col_at + col_step
    if 0 <= row_new < length and 0 <= col_new < length:
        return (face_id, row_new, col_new, -1)
    if row_new < 0:
        edge_id = 0
    elif row_new >= length:
        edge_id = 1
    elif col_new < 0:
        edge_id = 2
    else:
        edge_id = 3
    along_edge = col_at if edge_id < 2 else row_at
    partner, entered = edge_partner(face_id, edge_id)
    row_in, col_in = entry_pixel(entered, along_edge, length)
    return (partner, row_in, col_in, entered)


def neighbour_pixel(face_id, row_at, col_at, row_step, col_step, length):
    if row_step == 0 or col_step == 0:
        found = step_pixel(face_id, row_at, col_at, row_step, col_step, length)
        return (found[0], found[1], found[2])
    face_one, row_one, col_one, entered = step_pixel(face_id, row_at, col_at, row_step, 0, length)
    if entered >= 2:
        found = step_pixel(face_one, row_one, col_one, col_step, 0, length)
    else:
        found = step_pixel(face_one, row_one, col_one, 0, col_step, length)
    return (found[0], found[1], found[2])


def tile_slot(face_id, tile_row, tile_col, side_tiles):
    group_id = face_id // 4
    within = face_id % 4
    extra = 1 if group_id == 2 else 0
    column = (side_tiles * (within + extra) + tile_col) % (4 * side_tiles)
    return 3 * side_tiles * column + side_tiles * group_id + tile_row


def cycle_position(row_at, col_at, pixels):
    if row_at == 0:
        return col_at
    if row_at == pixels - 1:
        return pixels + col_at
    if col_at == 0:
        return 2 * pixels + row_at
    return 3 * pixels + row_at


def halo_positions(pixels):
    places = [(-1, column) for column in range(-1, pixels + 1)]
    places = places + [(pixels, column) for column in range(-1, pixels + 1)]
    places = places + [(row_at, -1) for row_at in range(pixels)]
    places = places + [(row_at, pixels) for row_at in range(pixels)]
    return places


def halo_sources(side_tiles, pixels):
    slot_count = 12 * side_tiles * side_tiles
    places = halo_positions(pixels)
    length = side_tiles * pixels
    source_slot = np.zeros((slot_count, len(places)), np.int64)
    source_cycle = np.zeros((slot_count, len(places)), np.int64)
    for face_id in range(12):
        for tile_row in range(side_tiles):
            for tile_col in range(side_tiles):
                slot_id = tile_slot(face_id, tile_row, tile_col, side_tiles)
                for cell_index in range(len(places)):
                    row_at, col_at = places[cell_index]
                    inner_row = min(max(row_at, 0), pixels - 1)
                    inner_col = min(max(col_at, 0), pixels - 1)
                    partner, row_new, col_new = neighbour_pixel(
                        face_id,
                        tile_row * pixels + inner_row,
                        tile_col * pixels + inner_col,
                        row_at - inner_row,
                        col_at - inner_col,
                        length,
                    )
                    source_slot[slot_id, cell_index] = tile_slot(
                        partner, row_new // pixels, col_new // pixels, side_tiles
                    )
                    source_cycle[slot_id, cell_index] = cycle_position(
                        row_new % pixels, col_new % pixels, pixels
                    )
    return (source_slot, source_cycle)


def halo_rows(row_at, col_at, pixels):
    if row_at == -1 or row_at == pixels:
        base = 0 if row_at == -1 else 3 * pixels
        return [
            base + pixels * shift + col_at + 1 - shift
            for shift in range(3)
            if 0 <= col_at + 1 - shift < pixels
        ]
    return [6 * pixels + row_at if col_at == -1 else 7 * pixels + row_at]


def outer_row(row_at, col_at, pixels):
    if col_at == -1:
        return 2 * pixels + row_at + 1
    if col_at == pixels:
        return 4 * pixels + row_at + 1
    return col_at if row_at == -1 else pixels + col_at


def device_tables(device_count, per_device, side_tiles, pixels):
    source_slot, source_cycle = halo_sources(side_tiles, pixels)
    places = halo_positions(pixels)
    rim_len, halo_len, outer_len = 4 * pixels, 8 * pixels, 6 * pixels
    sends = {}
    local = []
    for device in range(device_count):
        local.append([])
        for local_id in range(per_device):
            slot_id = device * per_device + local_id
            for cell in range(len(places)):
                row_at, col_at = places[cell]
                source = int(source_slot[slot_id, cell])
                moved_by = (device - source // per_device) % device_count
                if moved_by > device_count // 2:
                    moved_by -= device_count
                rim = source % per_device * rim_len + int(source_cycle[slot_id, cell])
                halo = [local_id * halo_len + h for h in halo_rows(row_at, col_at, pixels)]
                outer = local_id * outer_len + outer_row(row_at, col_at, pixels)
                record = (rim, halo, outer)
                if moved_by == 0:
                    local[device].append(record)
                else:
                    lists = sends.setdefault(moved_by, [[] for _ in range(device_count)])
                    lists[device].append(record)
    offsets = sorted(sends)
    widths = [-(-max(len(one) for one in sends[offset]) // 16) * 16 for offset in offsets]
    total = sum(widths)
    send = np.full((device_count, total), -1, np.int32)
    receive = np.full((device_count, per_device * halo_len), -1, np.int32)
    back = np.full((device_count, total), -1, np.int32)
    target = np.full((device_count, per_device * outer_len + total), -1, np.int32)
    for device in range(device_count):
        for rim, halo, outer in local[device]:
            receive[device, halo] = rim
            target[device, outer] = rim
        base = 0
        for offset, width in zip(offsets, widths):
            sender = (device - offset) % device_count
            for at, (rim, halo, outer) in enumerate(sends[offset][device]):
                send[sender, base + at] = rim
                receive[device, halo] = per_device * rim_len + base + at
                back[device, base + at] = outer
                target[sender, per_device * outer_len + base + at] = rim
            base += width
    return (offsets, widths, send, receive, back, target)


def one_hot(table_np, tile_index, width):
    row = jnp.asarray(table_np, dtype=jnp.int32)[tile_index]
    return (row[:, None] == lax.broadcasted_iota(jnp.int32, (row.shape[0], width), 1)).astype(
        jnp.bfloat16
    )


def exchanged(rows, offsets, widths, sign):
    pieces, base = [], 0
    for offset, width in zip(offsets, widths):
        pieces.append(passed_along(rows[base : base + width], "tile", sign * offset))
        base += width
    return pieces


def halo_of(rim, layout, tile_index):
    offsets, widths, send, receive = layout[:4]
    outgoing = jnp.dot(one_hot(send, tile_index, rim.shape[0]), rim)
    pool = jnp.concatenate([rim] + exchanged(outgoing, offsets, widths, 1), axis=0)
    return jnp.dot(one_hot(receive, tile_index, pool.shape[0]), pool)


def folded(outer, layout, tile_index, rim_rows):
    offsets, widths, _, _, back, target = layout
    outgoing = jnp.dot(one_hot(back, tile_index, outer.shape[0]), outer)
    pool = jnp.concatenate([outer] + exchanged(outgoing, offsets, widths, -1), axis=0)
    spread = one_hot(target, tile_index, rim_rows)
    return lax.dot_general(
        spread, pool, (((0,), (0,)), ((), ())), preferred_element_type=jnp.float32
    )


def gelu_parts(value):
    half = 0.5 * (1.0 + lax.erf(value * inv_sqrt_two))
    return value * half, half + value * jnp.exp(-0.5 * value * value) * inv_sqrt_tau


def columns_at(tile, halo, work, pixels):
    count = pixels * pixels
    wide = tile.astype(jnp.float32)
    halo_wide = halo[6 * pixels :].astype(jnp.float32)
    work[0, pl.ds(1, count - 1), :] = wide[: count - 1]
    work[0, pl.ds(0, pixels, stride=pixels), :] = halo_wide[:pixels]
    work[1, pl.ds(0, count - 1), :] = wide[1:]
    work[1, pl.ds(pixels - 1, pixels, stride=pixels), :] = halo_wide[pixels:]
    middles = [work[0].astype(jnp.bfloat16), tile, work[1].astype(jnp.bfloat16)]
    joined = jnp.concatenate(
        [
            jnp.concatenate(
                [
                    halo[pixels * b : pixels * (b + 1)],
                    middles[b],
                    halo[pixels * (3 + b) : pixels * (4 + b)],
                ],
                axis=0,
            )
            for b in range(3)
        ],
        axis=1,
    )
    return jnp.concatenate([joined[pixels * a : pixels * a + count] for a in range(3)], axis=1)


def first_kernel(x_ref, halo_ref, w_ref, bias_ref, hidden_ref, slope_ref, rim_ref, work):
    batch, pixels, channels = x_ref.shape[1], x_ref.shape[2], x_ref.shape[4]
    count = pixels * pixels
    for s in range(batch):
        lanes = slice(s * channels, (s + 1) * channels)
        tile = x_ref[0, s].reshape(count, channels)
        cols = columns_at(tile, halo_ref[0, :, lanes], work.at[pl.ds(2 * s, 2)], pixels)
        pre = jnp.dot(cols, w_ref[...], preferred_element_type=jnp.float32) + bias_ref[...]
        hidden, slope = gelu_parts(pre)
        slope_ref[0, s] = slope
        work[2 * batch + s] = hidden
        rounded = hidden.astype(jnp.bfloat16)
        hidden_ref[0, s] = rounded.reshape(pixels, pixels, channels)
        rim_ref[0, 0:pixels, lanes] = rounded[:pixels]
        rim_ref[0, pixels : 2 * pixels, lanes] = rounded[count - pixels :]
        for side in range(2):
            edge = work[2 * batch + s, pl.ds(side * (pixels - 1), pixels, stride=pixels), :]
            rim_ref[0, (2 + side) * pixels : (3 + side) * pixels, lanes] = edge.astype(jnp.bfloat16)


def second_kernel(
    x_ref, halo_ref, cot_ref, w_ref, flip_ref, side_ref, bias_ref,
    out_ref, inner_ref, outer_ref, grad_ref, sum_ref, work, cols_ref, delta_ref, edge_ref,
):
    batch, pixels, channels = x_ref.shape[1], x_ref.shape[2], x_ref.shape[4]
    count = pixels * pixels

    @pl.when(pl.program_id(0) == 0)
    def _():
        grad_ref[...] = jnp.zeros_like(grad_ref)
        sum_ref[...] = jnp.zeros_like(sum_ref)

    zero_row = jnp.zeros((1, channels), jnp.float32)
    zero_col = jnp.zeros((pixels, channels), jnp.float32)
    zeros = jnp.zeros((2 * pixels, 3 * channels), jnp.bfloat16)
    for s in range(batch):
        lanes = slice(s * channels, (s + 1) * channels)
        tile = x_ref[0, s].reshape(count, channels)
        here = work.at[pl.ds(2 * s, 2)]
        cols = columns_at(tile, halo_ref[0, :, lanes], here, pixels)
        cols_ref[s * count : (s + 1) * count, :] = cols
        pre = jnp.dot(cols, w_ref[...], preferred_element_type=jnp.float32) + bias_ref[...]
        value, slope = gelu_parts(pre)
        out_ref[0, s] = value.astype(jnp.bfloat16).reshape(pixels, pixels, channels)
        cot = cot_ref[0, s].reshape(count, channels).astype(jnp.float32)
        delta = (cot * slope).astype(jnp.bfloat16)
        delta_ref[s * count : (s + 1) * count, :] = delta
        wide = delta.astype(jnp.float32)
        sum_ref[...] += jnp.sum(wide, axis=0, keepdims=True)
        edge_ref[s] = jnp.zeros(edge_ref.shape[1:], jnp.float32)
        work[2 * batch + s] = wide
        for side in range(2):
            edge_ref[s, side, pl.ds(2, pixels), :] = work[
                2 * batch + s, pl.ds(side * (pixels - 1), pixels, stride=pixels), :
            ]
        here[0, pl.ds(0, count - 1), :] = wide[1:]
        here[0, pl.ds(pixels - 1, pixels, stride=pixels), :] = zero_col
        here[1, pl.ds(1, count - 1), :] = wide[: count - 1]
        here[1, pl.ds(0, pixels, stride=pixels), :] = zero_col
        joined = jnp.concatenate(
            [here[0].astype(jnp.bfloat16), delta, here[1].astype(jnp.bfloat16)], axis=1
        )
        joined = jnp.concatenate([zeros, joined, zeros], axis=0)
        tall = count + 2 * pixels
        spread = jnp.concatenate(
            [joined[pixels * (2 - a) : pixels * (2 - a) + tall] for a in range(3)], axis=1
        )
        grad = jnp.dot(spread, flip_ref[...], preferred_element_type=jnp.float32)
        inner_ref[0, s] = grad[pixels : pixels + count]
        outer_ref[0, 0:pixels, lanes] = grad[:pixels].astype(jnp.bfloat16)
        outer_ref[0, pixels : 2 * pixels, lanes] = grad[pixels + count :].astype(jnp.bfloat16)
        for side in range(2):
            lhs = jnp.concatenate(
                [edge_ref[s, side, pl.ds(2 - a, 2 * pixels), :] for a in range(3)], axis=1
            ).astype(jnp.bfloat16)
            part = jnp.dot(lhs, side_ref[side], preferred_element_type=jnp.float32)
            outer_ref[0, 2 * pixels * (1 + side) : 2 * pixels * (2 + side), lanes] = part.astype(
                jnp.bfloat16
            )
    grad_ref[...] += lax.dot_general(
        delta_ref[...], cols_ref[...], (((0,), (0,)), ((), ())), preferred_element_type=jnp.float32
    )


def third_kernel(
    x_ref, halo_ref, inner_ref, rim_ref, slope_ref, grad_ref, sum_ref, work, cols_ref, delta_ref
):
    batch, pixels, channels = x_ref.shape[1], x_ref.shape[2], x_ref.shape[4]
    count = pixels * pixels

    @pl.when(pl.program_id(0) == 0)
    def _():
        grad_ref[...] = jnp.zeros_like(grad_ref)
        sum_ref[...] = jnp.zeros_like(sum_ref)

    for s in range(batch):
        lanes = slice(s * channels, (s + 1) * channels)
        tile = x_ref[0, s].reshape(count, channels)
        cols_ref[s * count : (s + 1) * count, :] = columns_at(
            tile, halo_ref[0, :, lanes], work.at[pl.ds(2 * s, 2)], pixels
        )
        at = 2 * batch + s
        work[at] = inner_ref[0, s]
        work[at, pl.ds(0, pixels), :] += rim_ref[0, 0:pixels, lanes]
        work[at, pl.ds(count - pixels, pixels), :] += rim_ref[0, pixels : 2 * pixels, lanes]
        for side in range(2):
            place = pl.ds(side * (pixels - 1), pixels, stride=pixels)
            edge = rim_ref[0, (2 + side) * pixels : (3 + side) * pixels, lanes]
            work[at, place, :] = work[at, place, :] + edge
        delta = (work[at] * slope_ref[0, s]).astype(jnp.bfloat16)
        delta_ref[s * count : (s + 1) * count, :] = delta
        sum_ref[...] += jnp.sum(delta.astype(jnp.float32), axis=0, keepdims=True)
    grad_ref[...] += lax.dot_general(
        delta_ref[...], cols_ref[...], (((0,), (0,)), ((), ())), preferred_element_type=jnp.float32
    )


def per_tile(shape):
    return pl.BlockSpec((1,) + tuple(shape), lambda t: (t,) + (0,) * len(shape))


def whole(shape):
    return pl.BlockSpec(tuple(shape), lambda t: (0,) * len(shape))


params = dict(vmem_limit_bytes=48 * 1024 * 1024)


def body(features, weight_one, bias_one, weight_two, bias_two, cotangent):
    device_count = lax.axis_size("tile")
    samples_count = lax.axis_size("tm")
    tile_index = lax.axis_index("tile")
    per_device, batch, pixels, _, channels = features.shape
    count = pixels * pixels
    lane_count = batch * channels
    layout = device_tables(device_count, per_device, S, pixels)
    bf16, f32 = jnp.bfloat16, jnp.float32
    tile_shape = (batch, pixels, pixels, channels)
    flat_shape = (batch, count, channels)
    halo_shape = (8 * pixels, lane_count)
    rim_shape = (4 * pixels, lane_count)
    outer_shape = (6 * pixels, lane_count)
    mat_one = weight_one.reshape(9 * channels, channels)
    mat_two = weight_two.reshape(9 * channels, channels)
    turned = weight_two.transpose(0, 1, 3, 2)
    flip = turned.reshape(9 * channels, channels)
    sides = jnp.stack([turned[:, 0], turned[:, 2]]).reshape(2, 3 * channels, channels)

    def out(shape, dtype):
        return jax.ShapeDtypeStruct((per_device,) + tuple(shape), dtype)

    work = pltpu.VMEM((3 * batch, count, channels), f32)
    cols = pltpu.VMEM((batch * count, 9 * channels), bf16)
    deltas = pltpu.VMEM((batch * count, channels), bf16)
    grad_shape = (channels, 9 * channels)

    rim_one = jnp.concatenate(
        [features[:, :, 0], features[:, :, -1], features[:, :, :, 0], features[:, :, :, -1]], axis=2
    )
    rim_one = rim_one.transpose(0, 2, 1, 3).reshape(per_device * 4 * pixels, lane_count)
    halo_one = halo_of(rim_one, layout, tile_index).reshape((per_device,) + halo_shape)
    hidden, slope, rim_two = pl.pallas_call(
        first_kernel,
        grid=(per_device,),
        in_specs=[per_tile(tile_shape), per_tile(halo_shape), whole(mat_one.shape), whole((1, channels))],
        out_specs=[per_tile(tile_shape), per_tile(flat_shape), per_tile(rim_shape)],
        out_shape=[out(tile_shape, bf16), out(flat_shape, f32), out(rim_shape, bf16)],
        scratch_shapes=[work],
        compiler_params=pltpu.CompilerParams(**params),
    )(features, halo_one, mat_one, bias_one.reshape(1, channels))
    halo_two = halo_of(rim_two.reshape(-1, lane_count), layout, tile_index)
    output, inner, outer, grad_two, sum_two = pl.pallas_call(
        second_kernel,
        grid=(per_device,),
        in_specs=[
            per_tile(tile_shape), per_tile(halo_shape), per_tile(tile_shape), whole(mat_two.shape),
            whole(flip.shape), whole(sides.shape), whole((1, channels)),
        ],
        out_specs=[
            per_tile(tile_shape), per_tile(flat_shape), per_tile(outer_shape),
            whole(grad_shape), whole((1, channels)),
        ],
        out_shape=[
            out(tile_shape, bf16), out(flat_shape, f32), out(outer_shape, bf16),
            jax.ShapeDtypeStruct(grad_shape, f32), jax.ShapeDtypeStruct((1, channels), f32),
        ],
        scratch_shapes=[work, cols, deltas, pltpu.VMEM((batch, 2, 2 * pixels + 8, channels), f32)],
        compiler_params=pltpu.CompilerParams(**params),
    )(
        hidden, halo_two.reshape((per_device,) + halo_shape), cotangent, mat_two, flip, sides,
        bias_two.reshape(1, channels),
    )
    rim_grad = folded(outer.reshape(-1, lane_count), layout, tile_index, per_device * 4 * pixels)
    grad_one, sum_one = pl.pallas_call(
        third_kernel,
        grid=(per_device,),
        in_specs=[
            per_tile(tile_shape), per_tile(halo_shape), per_tile(flat_shape), per_tile(rim_shape),
            per_tile(flat_shape),
        ],
        out_specs=[whole(grad_shape), whole((1, channels))],
        out_shape=[jax.ShapeDtypeStruct(grad_shape, f32), jax.ShapeDtypeStruct((1, channels), f32)],
        scratch_shapes=[work, cols, deltas],
        compiler_params=pltpu.CompilerParams(**params),
    )(features, halo_one, inner, rim_grad.reshape((per_device,) + rim_shape), slope)

    total_pixels = 12 * S * S * count * batch * samples_count
    grad_scale = 1.0 / math.sqrt(total_pixels)
    devices = device_count * samples_count
    axes = ("tile", "tm")

    def summed(grad, bias):
        rows = jnp.concatenate([grad.reshape(-1, channels), bias], axis=0)
        used = rows.shape[0]
        chunk = -(-used // (8 * devices)) * 8
        rows = jnp.pad(rows, ((0, chunk * devices - used), (0, 0)))
        parts = lax.all_to_all(rows.reshape(devices, chunk, channels), axes, 0, 0)
        mine = (jnp.sum(parts, axis=0) * grad_scale).astype(bf16)
        copies = jnp.broadcast_to(mine[None], (devices, chunk, channels))
        total = lax.all_to_all(copies, axes, 0, 0).reshape(devices * chunk, channels).astype(f32)
        weight = total[: used - 1].reshape(channels, 3, 3, channels).transpose(1, 2, 3, 0)
        return weight, total[used - 1]

    grad_weight_two, grad_bias_two = summed(grad_two, sum_two)
    grad_weight_one, grad_bias_one = summed(grad_one, sum_one)
    return (output, grad_weight_one, grad_bias_one, grad_weight_two, grad_bias_two)


def solution(mesh):
    return jax.shard_map(
        body,
        mesh=mesh,
        in_specs=(
            P("tile", "tm", None, None, None),
            P(),
            P(),
            P(),
            P(),
            P("tile", "tm", None, None, None),
        ),
        out_specs=(P("tile", "tm", None, None, None), P(), P(), P(), P()),
        check_vma=False,
    )
```
